128 devices in a mesh: ctx: 32 (over y, z_hi, x), dp: 4 (over z_lo, core).
Axes of the slice: x: 4, y: 4, z: 4 (z_hi: 2, z_lo: 2; z = z_hi * 2 + z_lo), core: 2. Of those that a mesh axis runs over, the one named last changes fastest.
Arguments:
- queries: bfloat16 [4, 4096, 12288], P('dp', 'ctx'), may hold values from -6 to 6
- latents: bfloat16 [4, 4096, 576], P('dp', 'ctx'), may hold values from -6 to 6
- cotangent: bfloat16 [4, 4096, 8192], P('dp', 'ctx'), may hold values from -6 to 6
- offsets: float32 [4, 64, 4096], P('dp', None, 'ctx'), may hold values from 2 to 4
- corrections: float32 [4, 64, 4096], P('dp', None, 'ctx'), may hold values from -24 to 24
- span_order: int32 [4, 64], P('dp'), may hold values from 0 to 63, each once within a row
- latent_gain: float32 [512], replicated, may hold values from 0.1 to 1.9
- up_weight: bfloat16 [512, 16384], replicated, may hold values from -0.25 to 0.25
Outputs:
- grad_query: bfloat16 [4, 4096, 12288], P('dp', 'ctx')
- grad_latent: float32 [4, 4096, 576], P('dp', 'ctx')
- grad_gain: float32 [512], replicated
The draws below stay inside these ranges and needn't reach their ends.
Inputs may be any that keep to these rules, and one draw needn't show every extreme that they name: Each row of span_order names every block of the sequence exactly once.
All inputs are finite; a program needn't handle non-finite values.
Results may differ from the reference program's by a relative error of at most 0.012.
The reference program's roundings to bfloat16 on the way (of `scaled`, `projected` and `key_grads`) count: a program that leaves them out, or rounds other values in their place, can miss the bound.
Values may be sent and summed in bfloat16 or wider, within the bound.
No kernel may reach another device: no remote copies, remote signals or barrier semaphores. Data moves between devices by JAX's collectives and lax.ppermute only.
A program may use at most 256 MiB of HBM per device.

```python
import jax
import jax.numpy as jnp
from jax import lax

H = 64
KVL = 512
DR = 64
DN = 128
DV = 128
STEPS = 5
TOK_DEV = 128
SEQ = 4096
SEQS = 4
N_CTX = 32


def shard_levels(rng, dims, shards, low, high):
    level = 1.0
    for axis_at, parts in shards:
        draws = jax.random.uniform(jax.random.fold_in(jax.random.fold_in(rng, 6), axis_at), (parts,), jnp.float32, low / len(shards), high / len(shards))
        level = level * jnp.repeat(jnp.exp(draws), dims[axis_at] // parts).reshape((-1,) + (1,) * (len(dims) - 1 - axis_at))
    return level


def centred(own_key, dims, spread, bound, shards=(), kind=jnp.bfloat16):
    loudness = shard_levels(own_key, dims, shards, -0.22, 0.18) if shards else 1.0
    entries = jax.random.normal(own_key, dims, jnp.float32) * spread * loudness
    return jnp.minimum(jnp.maximum(entries, -bound), bound).astype(kind)


def setup_inputs(seed: int = 0) -> dict:
    arg_keys = jax.random.split(jax.random.key(seed), 9)
    return {
        "queries": centred(arg_keys[0], (SEQS, SEQ, H * (DN + DR)), 1.0, 6.0, ((0, 4), (1, 32))),
        "latents": centred(arg_keys[1], (SEQS, SEQ, KVL + DR), 1.0, 6.0, ((0, 4), (1, 32))),
        "cotangent": centred(arg_keys[2], (SEQS, SEQ, H * DV), 1.0, 6.0, ((0, 4), (1, 32))),
        "offsets": jnp.clip(2.0 + 2.0 * jax.random.uniform(arg_keys[3], (SEQS, H, SEQ), jnp.float32) ** shard_levels(arg_keys[3], (SEQS, H, SEQ), ((0, 4), (2, 32)), -0.2, 0.2), 2.0, 4.0),
        "corrections": centred(arg_keys[4], (SEQS, H, SEQ), 4.0, 24.0, ((0, 4), (2, 32)), jnp.float32),
        "span_order": jax.vmap(lambda own: jax.random.permutation(own, 2 * N_CTX))(jax.random.split(arg_keys[5], SEQS)).reshape((SEQS, 2 * N_CTX)).astype(jnp.int32),
        "latent_gain": jnp.clip(1.0 + 0.18 * jax.random.normal(arg_keys[6], (KVL,), jnp.float32), 0.1, 1.9),
        "up_weight": centred(arg_keys[7], (KVL, H * (DN + DV)), KVL ** -0.5, 0.25),
    }


def visit(own_queries, own_cotangent, own_offsets, own_corrections, query_pos, visitor, key_pos, latent_gain, up_weight):
    query_rows = own_queries.shape[0]
    key_rows = visitor.shape[0]
    score_scale = (DN + DR) ** -0.5
    scaled = (visitor[:, :KVL].astype(jnp.float32) * latent_gain[None, :]).astype(jnp.bfloat16)
    projected = jnp.dot(scaled, up_weight, preferred_element_type=jnp.float32).astype(jnp.bfloat16)
    projected = projected.reshape(key_rows, H, DN + DV).astype(jnp.float32)
    key_heads = projected[:, :, :DN]
    values = projected[:, :, DN:]
    rope_keys = visitor[:, KVL:].astype(jnp.float32)
    query_heads = own_queries.reshape(query_rows, H, DN + DR).astype(jnp.float32)
    query_nope = query_heads[:, :, :DN]
    rotary = query_heads[:, :, DN:]
    out_heads = own_cotangent.reshape(query_rows, H, DV).astype(jnp.float32)
    scores = (jnp.einsum("thd,uhd->htu", query_nope, key_heads) + jnp.einsum("thd,ud->htu", rotary, rope_keys)) * score_scale
    visible = key_pos[None, :] <= query_pos[:, None]
    probability = jnp.where(visible[None], jnp.exp(scores - own_offsets[:, :, None]), 0.0)
    prob_grad = jnp.einsum("thd,uhd->htu", out_heads, values)
    score_grad = probability * (prob_grad - own_corrections[:, :, None])
    rounded_prob = lax.optimization_barrier(probability.astype(jnp.bfloat16)).astype(jnp.float32)
    rounded_score = lax.optimization_barrier(score_grad.astype(jnp.bfloat16)).astype(jnp.float32)
    query_part = jnp.concatenate([jnp.einsum("htu,uhd->thd", rounded_score, key_heads), jnp.einsum("htu,ud->thd", rounded_score, rope_keys)], 2)
    query_part = query_part.reshape(query_rows, H * (DN + DR))
    key_part = (score_scale * jnp.einsum("htu,thd->uhd", rounded_score, query_nope)).astype(jnp.bfloat16)
    value_part = jnp.einsum("htu,thd->uhd", rounded_prob, out_heads).astype(jnp.bfloat16)
    key_grads = jnp.concatenate([key_part, value_part], 2).reshape(key_rows, H * (DN + DV))
    rotary_grad = score_scale * jnp.einsum("htu,thd->ud", rounded_score, rotary)
    latent_grad = jnp.concatenate([lax.dot_general(key_grads, up_weight, (((1,), (1,)), ((), ())), preferred_element_type=jnp.float32), rotary_grad], 1)
    return query_part, latent_grad


def reference(queries, latents, cotangent, offsets, corrections, span_order, latent_gain, up_weight):
    half_block = TOK_DEV // 2
    score_scale = (DN + DR) ** -0.5
    token_index = jnp.arange(SEQ, dtype=jnp.int32)
    gain_sum = jnp.zeros((KVL,), jnp.float32)
    query_out = []
    latent_out = []
    for sequence in range(SEQS):
        positions = span_order[sequence][token_index // half_block] * half_block + token_index % half_block

        def group_step(latent_acc, member):
            first_row = (member * TOK_DEV).astype(jnp.int32)
            own_queries = lax.dynamic_slice_in_dim(queries[sequence], first_row, TOK_DEV, 0)
            own_cotangent = lax.dynamic_slice_in_dim(cotangent[sequence], first_row, TOK_DEV, 0)
            own_offsets = lax.dynamic_slice_in_dim(offsets[sequence], first_row, TOK_DEV, 1)
            own_corrections = lax.dynamic_slice_in_dim(corrections[sequence], first_row, TOK_DEV, 1)
            query_pos = lax.dynamic_slice_in_dim(positions, first_row, TOK_DEV, 0)
            accumulated = jnp.zeros((TOK_DEV, H * (DN + DR)), jnp.float32)
            for cycle_step in range(STEPS):
                source = (member - cycle_step) % N_CTX
                key_start = (source * TOK_DEV).astype(jnp.int32)
                visitor = lax.dynamic_slice_in_dim(latents[sequence], key_start, TOK_DEV, 0)
                key_pos = lax.dynamic_slice_in_dim(positions, key_start, TOK_DEV, 0)
                query_part, latent_grad = visit(own_queries, own_cotangent, own_offsets, own_corrections, query_pos, visitor, key_pos, latent_gain, up_weight)
                accumulated = accumulated + query_part
                current = lax.dynamic_slice_in_dim(latent_acc, key_start, TOK_DEV, 0)
                latent_acc = lax.dynamic_update_slice_in_dim(latent_acc, current + latent_grad, key_start, 0)
            return latent_acc, (score_scale * accumulated).astype(jnp.bfloat16)

        start_latent = jnp.zeros((SEQ, KVL + DR), jnp.float32)
        latent_acc, query_grad = lax.scan(group_step, start_latent, jnp.arange(N_CTX, dtype=jnp.int32))
        gain_sum = gain_sum + jnp.sum(latents[sequence][:, :KVL].astype(jnp.float32) * latent_acc[:, :KVL], axis=0)
        query_out.append(query_grad.reshape(SEQ, H * (DN + DR)))
        latent_out.append(jnp.concatenate([latent_gain[None, :] * latent_acc[:, :KVL], latent_acc[:, KVL:]], 1))
    return jnp.stack(query_out), jnp.stack(latent_out), gain_sum
```

```python
import functools
import jax
import jax.numpy as jnp
from jax import lax
from jax.experimental import pallas as pl
from jax.experimental.pallas import tpu as pltpu
from jax.sharding import PartitionSpec as P

H = 64
KVL = 512
DR = 64
DN = 128
DV = 128
STEPS = 5
HB = 2
TOK = 128
N_CTX = 32
SCALE = (DN + DR) ** -0.5
LOG2E = 1.4426950408889634
F32 = jnp.float32
BF16 = jnp.bfloat16


def dot_t(a, b):
    return lax.dot_general(a, b, (((1,), (1,)), ((), ())), preferred_element_type=F32)


def dot_l(a, b):
    return lax.dot_general(a, b, (((0,), (0,)), ((), ())), preferred_element_type=F32)


def dot_n(a, b):
    return jnp.dot(a, b, preferred_element_type=F32)


def kernel(steps, order, member, gain, offs, corr, *refs):
    n = len(steps)
    lats = refs[:n]
    w, q, cot, dq = refs[n : n + 4]
    grads = refs[n + 4 : 2 * n + 4]
    gain_part = refs[2 * n + 4]
    scaled, rope, bias, acc, racc, mul = refs[2 * n + 5 :]
    step = pl.program_id(0)
    half = TOK // 2

    @pl.when(step == 0)
    def _():
        rows = lax.broadcasted_iota(jnp.int32, (TOK, TOK), 0)
        cols = lax.broadcasted_iota(jnp.int32, (TOK, TOK), 1)
        own = member[0]

        def positions(index, group):
            block = jnp.where(index < half, order[0, 2 * group], order[0, 2 * group + 1])
            return block * half + lax.rem(index, half)

        qpos = positions(cols, own)
        for i, s in enumerate(steps):
            group = lax.rem(own + N_CTX - s, N_CTX)
            kpos = positions(rows, group)
            part = pl.ds(i * TOK, TOK)
            bias[part, :] = jnp.where(kpos <= qpos, 0.0, -1e30)
            tile = lats[i][...].astype(F32).T
            scaled[part, :] = (tile[:, :KVL] * gain[...]).astype(BF16)
            rope[part, :] = tile[:, KVL:].astype(BF16)
        acc[...] = jnp.zeros_like(acc)
        racc[...] = jnp.zeros_like(racc)

    rot = jnp.concatenate([q[:, DN : DN + DR], q[:, 2 * DN + DR :]], 0)
    proj = dot_n(scaled[...], w[...]).astype(BF16)
    srot = dot_t(rope[...], rot)
    zero = jnp.zeros((TOK, TOK), BF16)
    dss, dkvs = [], []
    for i in range(HB):
        qn = q[:, i * (DN + DR) : i * (DN + DR) + DN]
        ct = cot[:, i * DV : (i + 1) * DV]
        diag = jnp.concatenate(
            [jnp.concatenate([qn, zero], 1), jnp.concatenate([zero, ct], 1)], 0
        )
        head = step * HB + i
        off = offs[pl.ds(head, 1), :] * LOG2E
        cor = corr[pl.ds(head, 1), :]
        ph = proj[:, i * 256 : (i + 1) * 256]
        sd = dot_t(ph, diag)
        s = sd[:, :TOK] + srot[:, i * TOK : (i + 1) * TOK]
        p = jnp.exp2(s * (SCALE * LOG2E) + (bias[...] - off))
        ds = (p * (sd[:, TOK:] - cor)).astype(BF16)
        pb = p.astype(BF16)
        dkv = dot_n(jnp.concatenate([ds, pb], 1), diag)
        dkvs.append((dkv * mul[...]).astype(BF16))
        dss.append(ds)
        kr = jnp.concatenate([ph[:, :DN], rope[...]], 1)
        dq[:, i * (DN + DR) : (i + 1) * (DN + DR)] = (dot_l(ds, kr) * SCALE).astype(BF16)
    racc[...] += dot_n(jnp.concatenate(dss, 1), rot)
    acc[...] += dot_t(jnp.concatenate(dkvs, 1), w[...])

    @pl.when(step == H // HB - 1)
    def _():
        total = jnp.zeros((1, KVL), F32)
        for i in range(n):
            part = pl.ds(i * TOK, TOK)
            g = acc[part, :]
            tile = lats[i][:KVL, :].astype(F32).T
            total = total + jnp.sum(g * tile, axis=0, keepdims=True)
            grads[i][:KVL, :] = g.T
            grads[i][KVL:, :] = (racc[part, :] * SCALE).T
        gain_part[...] = total


def visits(steps, order, member, gain, offs, corr, lats, w, q, cot):
    n = len(steps)
    rows = n * TOK
    vm = pl.BlockSpec(memory_space=pltpu.VMEM)
    sm = pl.BlockSpec(memory_space=pltpu.SMEM)
    mul = jnp.concatenate([jnp.full((1, DN), SCALE, F32), jnp.ones((1, DV), F32)], 1)
    full = lambda *s: pl.BlockSpec(s, lambda i: (0,) * len(s))
    return pl.pallas_call(
        functools.partial(kernel_mul, steps),
        grid=(H // HB,),
        out_shape=[jax.ShapeDtypeStruct((TOK, H * (DN + DR)), BF16)]
        + [jax.ShapeDtypeStruct((KVL + DR, TOK), F32)] * n
        + [jax.ShapeDtypeStruct((1, KVL), F32)],
        in_specs=[sm, sm, full(1, KVL), full(H, TOK), full(H, TOK)]
        + [full(KVL + DR, TOK)] * n
        + [
            pl.BlockSpec((KVL, HB * (DN + DV)), lambda i: (0, i)),
            pl.BlockSpec((TOK, HB * (DN + DR)), lambda i: (0, i)),
            pl.BlockSpec((TOK, HB * DV), lambda i: (0, i)),
            full(1, DN + DV),
        ],
        out_specs=[pl.BlockSpec((TOK, HB * (DN + DR)), lambda i: (0, i))]
        + [full(KVL + DR, TOK)] * n
        + [full(1, KVL)],
        scratch_shapes=[
            pltpu.VMEM((rows, KVL), BF16),
            pltpu.VMEM((rows, DR), BF16),
            pltpu.VMEM((rows, TOK), F32),
            pltpu.VMEM((rows, KVL), F32),
            pltpu.VMEM((rows, DR), F32),
        ],
        compiler_params=pltpu.CompilerParams(vmem_limit_bytes=60 * 2**20, dimension_semantics=("arbitrary",)),
    )(order, member, gain, offs, corr, *lats, w, q, cot, mul)


def kernel_mul(steps, *refs):
    n = len(steps)
    mul = refs[5 + n + 3]
    rest = refs[: 5 + n + 3] + refs[5 + n + 4 :]
    kernel(steps, *rest, mul)


def xor_sum(x, bits):
    parts = [x]
    for bit in bits:
        parts = parts + [
            lax.ppermute(x, "ctx", [(i, i ^ (bit ^ done)) for i in range(lax.axis_size("ctx"))])
            for done in shifts(bits, bit)
        ]
    while len(parts) > 1:
        parts = [a + b for a, b in zip(parts[::2], parts[1::2])]
    return parts[0]


def shifts(bits, bit):
    low = [0]
    for other in bits:
        if other == bit:
            break
        low = low + [v ^ other for v in low]
    return low


def moved(x, distance):
    n = lax.axis_size("ctx")
    return lax.ppermute(x, "ctx", [((i - distance) % n, i) for i in range(n)])


def body(queries, latents, cotangent, offsets, corrections, span_order, latent_gain, up_weight):
    own = latents[0].T
    member = lax.axis_index("ctx").astype(jnp.int32).reshape(1)
    lats = [own] + [moved(own, s) for s in range(1, STEPS)]
    dq, *grads, gain_part = visits(
        tuple(range(STEPS)),
        span_order,
        member,
        latent_gain[None],
        offsets[0],
        corrections[0],
        lats,
        up_weight,
        queries[0],
        cotangent[0],
    )
    back = [moved(grads[s], -s) for s in range(1, STEPS)]
    gain_sum = lax.psum(gain_part[0], "dp")
    for bits in ((1, 2), (4,), (8, 16)):
        gain_sum = xor_sum(gain_sum, bits)
    total = grads[0] + ((back[0] + back[1]) + (back[2] + back[3]))
    factor = jnp.concatenate([latent_gain, jnp.ones((DR,), F32)])
    return dq[None], (total * factor[:, None]).T[None], gain_sum


def solution(mesh):
    in_specs = (
        P("dp", "ctx", None),
        P("dp", "ctx", None),
        P("dp", "ctx", None),
        P("dp", None, "ctx"),
        P("dp", None, "ctx"),
        P("dp", None),
        P(),
        P(),
    )
    out_specs = (P("dp", "ctx", None), P("dp", "ctx", None), P())
    return jax.shard_map(body, mesh=mesh, in_specs=in_specs, out_specs=out_specs, check_vma=False)
```

```python
import functools
import jax
import jax.numpy as jnp
from jax import lax
from jax.experimental import pallas as pl
from jax.experimental.pallas import tpu as pltpu
from jax.sharding import PartitionSpec as P

H = 64
KVL = 512
DR = 64
DN = 128
DV = 128
STEPS = 5
HB = 8
TOK = 128
N_CTX = 32
SCALE = (DN + DR) ** -0.5
LOG2E = 1.4426950408889634
F32 = jnp.float32
BF16 = jnp.bfloat16


def dot_t(a, b):
    return lax.dot_general(a, b, (((1,), (1,)), ((), ())), preferred_element_type=F32)


def dot_l(a, b):
    return lax.dot_general(a, b, (((0,), (0,)), ((), ())), preferred_element_type=F32)


def dot_n(a, b):
    return jnp.dot(a, b, preferred_element_type=F32)


def kernel(steps, order, member, gain, offs, corr, *refs):
    n = len(steps)
    lats = refs[:n]
    w, q, cot, dq = refs[n : n + 4]
    grads = refs[n + 4 : 2 * n + 4]
    gain_part = refs[2 * n + 4]
    scaled, rope, bias, acc, racc, mul = refs[2 * n + 5 :]
    step = pl.program_id(0)
    half = TOK // 2

    @pl.when(step == 0)
    def _():
        rows = lax.broadcasted_iota(jnp.int32, (TOK, TOK), 0)
        cols = lax.broadcasted_iota(jnp.int32, (TOK, TOK), 1)
        own = member[0]

        def positions(index, group):
            block = jnp.where(index < half, order[0, 2 * group], order[0, 2 * group + 1])
            return block * half + lax.rem(index, half)

        qpos = positions(cols, own)
        for i, s in enumerate(steps):
            group = lax.rem(own + N_CTX - s, N_CTX)
            kpos = positions(rows, group)
            part = pl.ds(i * TOK, TOK)
            bias[part, :] = jnp.where(kpos <= qpos, 0.0, -1e30)
            tile = lats[i][...].astype(F32).T
            scaled[part, :] = (tile[:, :KVL] * gain[...]).astype(BF16)
            rope[part, :] = tile[:, KVL:].astype(BF16)
        acc[...] = jnp.zeros_like(acc)
        racc[...] = jnp.zeros_like(racc)

    zero = jnp.zeros((TOK, TOK), BF16)
    proj = dot_n(scaled[...], w[...]).astype(BF16)
    dkvs = []
    rtotal = None
    for pair in range(HB // 2):
        base = 2 * pair * (DN + DR)
        rot = jnp.concatenate(
            [q[:, base + DN : base + DN + DR], q[:, base + 2 * DN + DR : base + 2 * (DN + DR)]], 0
        )
        srot = dot_t(rope[...], rot)
        pp = proj[:, pair * 512 : (pair + 1) * 512]
        dss = []
        for j in range(2):
            i = 2 * pair + j
            qn = q[:, i * (DN + DR) : i * (DN + DR) + DN]
            ct = cot[:, i * DV : (i + 1) * DV]
            diag = jnp.concatenate(
                [jnp.concatenate([qn, zero], 1), jnp.concatenate([zero, ct], 1)], 0
            )
            head = step * HB + i
            off = offs[pl.ds(head, 1), :] * LOG2E
            cor = corr[pl.ds(head, 1), :]
            ph = pp[:, j * 256 : (j + 1) * 256]
            sd = dot_t(ph, diag)
            s = sd[:, :TOK] + srot[:, j * TOK : (j + 1) * TOK]
            p = jnp.exp2(s * (SCALE * LOG2E) + (bias[...] - off))
            ds = (p * (sd[:, TOK:] - cor)).astype(BF16)
            pb = p.astype(BF16)
            dkv = dot_n(jnp.concatenate([ds, pb], 1), diag)
            dkvs.append((dkv * mul[...]).astype(BF16))
            dss.append(ds)
            kr = jnp.concatenate([ph[:, :DN], rope[...]], 1)
            dq[:, i * (DN + DR) : (i + 1) * (DN + DR)] = (dot_l(ds, kr) * SCALE).astype(BF16)
        rpart = dot_n(jnp.concatenate(dss, 1), rot)
        rtotal = rpart if rtotal is None else rtotal + rpart
    racc[...] += rtotal
    acc[...] += dot_t(jnp.concatenate(dkvs, 1), w[...])

    @pl.when(step == H // HB - 1)
    def _():
        total = jnp.zeros((1, KVL), F32)
        for i in range(n):
            part = pl.ds(i * TOK, TOK)
            g = acc[part, :]
            tile = lats[i][:KVL, :].astype(F32).T
            total = total + jnp.sum(g * tile, axis=0, keepdims=True)
            grads[i][:KVL, :] = g.T.astype(grads[i].dtype)
            grads[i][KVL:, :] = (racc[part, :] * SCALE).T.astype(grads[i].dtype)
        gain_part[...] = total


def visits(steps, order, member, gain, offs, corr, lats, w, q, cot):
    n = len(steps)
    rows = n * TOK
    vm = pl.BlockSpec(memory_space=pltpu.VMEM)
    sm = pl.BlockSpec(memory_space=pltpu.SMEM)
    mul = jnp.concatenate([jnp.full((1, DN), SCALE, F32), jnp.ones((1, DV), F32)], 1)
    full = lambda *s: pl.BlockSpec(s, lambda i: (0,) * len(s))
    return pl.pallas_call(
        functools.partial(kernel_mul, steps),
        grid=(H // HB,),
        out_shape=[jax.ShapeDtypeStruct((TOK, H * (DN + DR)), BF16)]
        + [jax.ShapeDtypeStruct((KVL + DR, TOK), BF16 if s else F32) for s in steps]
        + [jax.ShapeDtypeStruct((1, KVL), F32)],
        in_specs=[sm, sm, full(1, KVL), full(H, TOK), full(H, TOK)]
        + [full(KVL + DR, TOK)] * n
        + [
            pl.BlockSpec((KVL, HB * (DN + DV)), lambda i: (0, i)),
            pl.BlockSpec((TOK, HB * (DN + DR)), lambda i: (0, i)),
            pl.BlockSpec((TOK, HB * DV), lambda i: (0, i)),
            full(1, DN + DV),
        ],
        out_specs=[pl.BlockSpec((TOK, HB * (DN + DR)), lambda i: (0, i))]
        + [full(KVL + DR, TOK)] * n
        + [full(1, KVL)],
        scratch_shapes=[
            pltpu.VMEM((rows, KVL), BF16),
            pltpu.VMEM((rows, DR), BF16),
            pltpu.VMEM((rows, TOK), F32),
            pltpu.VMEM((rows, KVL), F32),
            pltpu.VMEM((rows, DR), F32),
        ],
        compiler_params=pltpu.CompilerParams(vmem_limit_bytes=60 * 2**20, dimension_semantics=("arbitrary",)),
    )(order, member, gain, offs, corr, *lats, w, q, cot, mul)


def kernel_mul(steps, *refs):
    n = len(steps)
    mul = refs[5 + n + 3]
    rest = refs[: 5 + n + 3] + refs[5 + n + 4 :]
    kernel(steps, *rest, mul)


def everywhere_sum(row):
    count = lax.axis_size("ctx") * lax.axis_size("dp")
    rows = jnp.broadcast_to(row, (count, row.shape[1]))
    return jnp.sum(lax.all_to_all(rows, ("ctx", "dp"), 0, 0, tiled=True), 0)


def moved(x, distance):
    n = lax.axis_size("ctx")
    return lax.ppermute(x, "ctx", [((i - distance) % n, i) for i in range(n)])


def body(queries, latents, cotangent, offsets, corrections, span_order, latent_gain, up_weight):
    own = latents[0].T
    member = lax.axis_index("ctx").astype(jnp.int32).reshape(1)
    lats = [own] + [moved(own, s) for s in range(1, STEPS)]
    dq, *grads, gain_part = visits(
        tuple(range(STEPS)),
        span_order,
        member,
        latent_gain[None],
        offsets[0],
        corrections[0],
        lats,
        up_weight,
        queries[0],
        cotangent[0],
    )
    back = [moved(grads[s], -s) for s in range(1, STEPS)]
    gain_sum = everywhere_sum(gain_part)
    back = [b.astype(F32) for b in back]
    total = grads[0] + ((back[0] + back[1]) + (back[2] + back[3]))
    factor = jnp.concatenate([latent_gain, jnp.ones((DR,), F32)])
    return dq[None], (total * factor[:, None]).T[None], gain_sum


def solution(mesh):
    in_specs = (
        P("dp", "ctx", None),
        P("dp", "ctx", None),
        P("dp", "ctx", None),
        P("dp", None, "ctx"),
        P("dp", None, "ctx"),
        P("dp", None),
        P(),
        P(),
    )
    out_specs = (P("dp", "ctx", None), P("dp", "ctx", None), P())
    return jax.shard_map(body, mesh=mesh, in_specs=in_specs, out_specs=out_specs, check_vma=False)
```

```python
import functools
import jax
import jax.numpy as jnp
from jax import lax
from jax.experimental import pallas as pl
from jax.experimental.pallas import tpu as pltpu
from jax.sharding import PartitionSpec as P

H = 64
KVL = 512
DR = 64
DN = 128
DV = 128
STEPS = 5
HB = 8
LATER = 4
TOK = 128
N_CTX = 32
SCALE = (DN + DR) ** -0.5
LOG2E = 1.4426950408889634
F32 = jnp.float32
BF16 = jnp.bfloat16


def dot_t(a, b):
    return lax.dot_general(a, b, (((1,), (1,)), ((), ())), preferred_element_type=F32)


def dot_l(a, b):
    return lax.dot_general(a, b, (((0,), (0,)), ((), ())), preferred_element_type=F32)


def dot_n(a, b):
    return jnp.dot(a, b, preferred_element_type=F32)


def copy_out(step, slot, held, stored, sem):
    return pltpu.make_async_copy(held.at[slot], stored.at[step], sem.at[slot])


def kernel(steps, order, member, gain, mul, offs, corr, *refs):
    n = len(steps)
    lats = refs[:n]
    w, q, cot, dq, stored, rope = refs[n : n + 6]
    grads = refs[n + 6 : 2 * n + 6]
    gain_rows = refs[2 * n + 6]
    scaled, bias, acc, racc, held, sem = refs[2 * n + 7 :]
    step = pl.program_id(0)
    half = TOK // 2

    @pl.when(step == 0)
    def _():
        rows = lax.broadcasted_iota(jnp.int32, (TOK, TOK), 0)
        cols = lax.broadcasted_iota(jnp.int32, (TOK, TOK), 1)
        own = member[0]

        def positions(index, group):
            block = jnp.where(index < half, order[0, 2 * group], order[0, 2 * group + 1])
            return block * half + lax.rem(index, half)

        qpos = positions(cols, own)
        for i, s in enumerate(steps):
            group = lax.rem(own + N_CTX - s, N_CTX)
            kpos = positions(rows, group)
            part = pl.ds(i * TOK, TOK)
            bias[part, :] = jnp.where(kpos <= qpos, 0.0, -1e30)
            tile = lats[i][...].astype(F32).T
            scaled[part, :] = (tile[:, :KVL] * gain[...]).astype(BF16)
            rope[part, :] = tile[:, KVL:].astype(BF16)
        acc[...] = jnp.zeros_like(acc)
        racc[...] = jnp.zeros_like(racc)

    def heads(slot):
        zero = jnp.zeros((TOK, TOK), BF16)
        proj = dot_n(scaled[...], w[...]).astype(BF16)
        dkvs = []
        rtotal = None
        for pair in range(HB // 2):
            base = 2 * pair * (DN + DR)
            rot = jnp.concatenate(
                [q[:, base + DN : base + DN + DR], q[:, base + 2 * DN + DR : base + 2 * (DN + DR)]], 0
            )
            srot = dot_t(rope[...], rot)
            dss = []
            for j in range(2):
                i = 2 * pair + j
                qn = q[:, i * (DN + DR) : i * (DN + DR) + DN]
                ct = cot[:, i * DV : (i + 1) * DV]
                diag = jnp.concatenate(
                    [jnp.concatenate([qn, zero], 1), jnp.concatenate([zero, ct], 1)], 0
                )
                head = step * HB + i
                off = offs[pl.ds(head, 1), :] * LOG2E
                cor = corr[pl.ds(head, 1), :]
                ph = proj[:, i * (DN + DV) : (i + 1) * (DN + DV)]
                sd = dot_t(ph, diag)
                s = sd[:, :TOK] + srot[:, j * TOK : (j + 1) * TOK]
                p = jnp.exp2(s * (SCALE * LOG2E) + (bias[...] - off))
                ds = (p * (sd[:, TOK:] - cor)).astype(BF16)
                pb = p.astype(BF16)
                dkv = dot_n(jnp.concatenate([ds, pb], 1), diag)
                dkvs.append((dkv * mul[...]).astype(BF16))
                dss.append(ds)
                if slot is None:
                    kr = jnp.concatenate([ph[:, :DN], rope[...]], 1)
                    dq[:, i * (DN + DR) : (i + 1) * (DN + DR)] = (dot_l(ds, kr) * SCALE).astype(BF16)
                else:
                    held[slot, 2 * i] = ds
                    held[slot, 2 * i + 1] = ph[:, :DN]
            rpart = dot_n(jnp.concatenate(dss, 1), rot)
            rtotal = rpart if rtotal is None else rtotal + rpart
        racc[...] += rtotal
        acc[...] += dot_t(jnp.concatenate(dkvs, 1), w[...])

    slot = lax.rem(step, 2)

    @pl.when(jnp.logical_and(step >= 2, step < LATER + 2))
    def _():
        copy_out(step - 2, slot, held, stored, sem).wait()

    @pl.when(step < LATER)
    def _():
        heads(slot)
        copy_out(step, slot, held, stored, sem).start()

    @pl.when(step >= LATER)
    def _():
        heads(None)

    @pl.when(step == H // HB - 1)
    def _():
        total = jnp.zeros((1, KVL), F32)
        for i in range(n):
            part = pl.ds(i * TOK, TOK)
            g = acc[part, :]
            tile = lats[i][:KVL, :].astype(F32).T
            total = total + jnp.sum(g * tile, axis=0, keepdims=True)
            grads[i][:KVL, :] = g.T.astype(grads[i].dtype)
            grads[i][KVL:, :] = (racc[part, :] * SCALE).T.astype(grads[i].dtype)
        gain_rows[...] = jnp.broadcast_to(total[None], gain_rows.shape)


def later_kernel(stored, rope, _, dq):
    for i in range(HB):
        kr = jnp.concatenate([stored[0, 2 * i + 1], rope[...]], 1)
        dq[:, i * (DN + DR) : (i + 1) * (DN + DR)] = (dot_l(stored[0, 2 * i], kr) * SCALE).astype(BF16)


def later_queries(stored, rope, dq):
    rows = stored.shape[2]
    return pl.pallas_call(
        later_kernel,
        grid=(LATER,),
        out_shape=jax.ShapeDtypeStruct(dq.shape, dq.dtype),
        in_specs=[
            pl.BlockSpec((1, 2 * HB, rows, TOK), lambda i: (i, 0, 0, 0)),
            pl.BlockSpec((rows, DR), lambda i: (0, 0)),
            pl.BlockSpec(memory_space=pl.ANY),
        ],
        out_specs=pl.BlockSpec((TOK, HB * (DN + DR)), lambda i: (0, i)),
        input_output_aliases={2: 0},
        compiler_params=pltpu.CompilerParams(vmem_limit_bytes=40 * 2**20),
        cost_estimate=pl.CostEstimate(
            flops=2 * LATER * HB * TOK * rows * (DN + DR),
            bytes_accessed=LATER * HB * TOK * (4 * rows + 2 * (DN + DR)),
            transcendentals=0,
        ),
    )(stored, rope, dq)


def visits(steps, order, member, gain, offs, corr, lats, w, q, cot, peers):
    n = len(steps)
    rows = n * TOK
    sm = pl.BlockSpec(memory_space=pltpu.SMEM)
    mul = jnp.concatenate([jnp.full((1, DN), SCALE, F32), jnp.ones((1, DV), F32)], 1)
    full = lambda *s: pl.BlockSpec(s, lambda i: (0,) * len(s))
    return pl.pallas_call(
        functools.partial(kernel, steps),
        grid=(H // HB,),
        out_shape=[
            jax.ShapeDtypeStruct((TOK, H * (DN + DR)), BF16),
            jax.ShapeDtypeStruct((LATER, 2 * HB, rows, TOK), BF16),
            jax.ShapeDtypeStruct((rows, DR), BF16),
        ]
        + [jax.ShapeDtypeStruct((KVL + DR, TOK), BF16 if s else F32) for s in steps]
        + [jax.ShapeDtypeStruct((peers, 1, KVL), F32)],
        in_specs=[sm, sm, full(1, KVL), full(1, DN + DV), full(H, TOK), full(H, TOK)]
        + [full(KVL + DR, TOK)] * n
        + [
            pl.BlockSpec((KVL, HB * (DN + DV)), lambda i: (0, i)),
            pl.BlockSpec((TOK, HB * (DN + DR)), lambda i: (0, i)),
            pl.BlockSpec((TOK, HB * DV), lambda i: (0, i)),
        ],
        out_specs=[
            pl.BlockSpec((TOK, HB * (DN + DR)), lambda i: (0, jnp.maximum(i, LATER))),
            pl.BlockSpec(memory_space=pl.ANY),
            full(rows, DR),
        ]
        + [full(KVL + DR, TOK)] * n
        + [full(peers, 1, KVL)],
        scratch_shapes=[
            pltpu.VMEM((rows, KVL), BF16),
            pltpu.VMEM((rows, TOK), F32),
            pltpu.VMEM((rows, KVL), F32),
            pltpu.VMEM((rows, DR), F32),
            pltpu.VMEM((2, 2 * HB, rows, TOK), BF16),
            pltpu.SemaphoreType.DMA((2,)),
        ],
        compiler_params=pltpu.CompilerParams(vmem_limit_bytes=60 * 2**20),
    )(order, member, gain, mul, offs, corr, *lats, w, q, cot)


def everywhere_sum(rows):
    moved_rows = lax.all_to_all(rows, ("ctx", "dp"), 0, 0, tiled=True)
    return jnp.sum(moved_rows, (0, 1))


def moved(x, distance):
    n = lax.axis_size("ctx")
    return lax.ppermute(x, "ctx", [((i - distance) % n, i) for i in range(n)])


def body(queries, latents, cotangent, offsets, corrections, span_order, latent_gain, up_weight):
    own = latents[0].T
    member = lax.axis_index("ctx").astype(jnp.int32).reshape(1)
    lats = [own] + [moved(own, s) for s in range(1, STEPS)]
    dq, stored, rope, *grads, gain_rows = visits(
        tuple(range(STEPS)),
        span_order,
        member,
        latent_gain[None],
        offsets[0],
        corrections[0],
        lats,
        up_weight,
        queries[0],
        cotangent[0],
        lax.axis_size("ctx") * lax.axis_size("dp"),
    )
    back = [moved(grads[s], -s) for s in range(1, STEPS)]
    gain_sum = everywhere_sum(gain_rows)
    dq = later_queries(stored, rope, dq)
    back = [b.astype(F32) for b in back]
    total = grads[0] + ((back[0] + back[1]) + (back[2] + back[3]))
    factor = jnp.concatenate([latent_gain, jnp.ones((DR,), F32)])
    return dq[None], (total * factor[:, None]).T[None], gain_sum


def solution(mesh):
    in_specs = (
        P("dp", "ctx", None),
        P("dp", "ctx", None),
        P("dp", "ctx", None),
        P("dp", None, "ctx"),
        P("dp", None, "ctx"),
        P("dp", None),
        P(),
        P(),
    )
    out_specs = (P("dp", "ctx", None), P("dp", "ctx", None), P())
    return jax.shard_map(body, mesh=mesh, in_specs=in_specs, out_specs=out_specs, check_vma=False)
```

```python
import functools
import jax
import jax.numpy as jnp
from jax import lax
from jax.experimental import pallas as pl
from jax.experimental.pallas import tpu as pltpu
from jax.sharding import PartitionSpec as P

H = 64
KVL = 512
DR = 64
DN = 128
DV = 128
STEPS = 5
HB = 8
LATER = 6
EARLY = 3
TOK = 128
N_CTX = 32
SCALE = (DN + DR) ** -0.5
LOG2E = 1.4426950408889634
F32 = jnp.float32
BF16 = jnp.bfloat16


def dot_t(a, b):
    return lax.dot_general(a, b, (((1,), (1,)), ((), ())), preferred_element_type=F32)


def dot_l(a, b):
    return lax.dot_general(a, b, (((0,), (0,)), ((), ())), preferred_element_type=F32)


def dot_n(a, b):
    return jnp.dot(a, b, preferred_element_type=F32)


def arrange(steps, order, member, gain, lats, scaled, rope, bias):
    half = TOK // 2
    rows = lax.broadcasted_iota(jnp.int32, (TOK, TOK), 0)
    cols = lax.broadcasted_iota(jnp.int32, (TOK, TOK), 1)
    own = member[0]

    def positions(index, group):
        block = jnp.where(index < half, order[0, 2 * group], order[0, 2 * group + 1])
        return block * half + lax.rem(index, half)

    qpos = positions(cols, own)
    for i, s in enumerate(steps):
        group = lax.rem(own + N_CTX - s, N_CTX)
        kpos = positions(rows, group)
        part = pl.ds(i * TOK, TOK)
        bias[part, :] = jnp.where(kpos <= qpos, 0.0, -1e30)
        tile = lats[i][...].astype(F32).T
        scaled[part, :] = (tile[:, :KVL] * gain[...]).astype(BF16)
        rope[part, :] = tile[:, KVL:].astype(BF16)


def heads(step, part, refs, keep, dq):
    mul, offs, corr, w, q, cot, scaled, rope, bias, acc, racc = refs
    zero = jnp.zeros((TOK, TOK), BF16)
    proj = dot_n(scaled[part, :], w[...]).astype(BF16)
    dkvs = []
    rtotal = None
    for pair in range(HB // 2):
        base = 2 * pair * (DN + DR)
        rot = jnp.concatenate(
            [q[:, base + DN : base + DN + DR], q[:, base + 2 * DN + DR : base + 2 * (DN + DR)]], 0
        )
        srot = dot_t(rope[part, :], rot)
        dss = []
        for j in range(2):
            i = 2 * pair + j
            qn = q[:, i * (DN + DR) : i * (DN + DR) + DN]
            ct = cot[:, i * DV : (i + 1) * DV]
            diag = jnp.concatenate(
                [jnp.concatenate([qn, zero], 1), jnp.concatenate([zero, ct], 1)], 0
            )
            head = step * HB + i
            off = offs[pl.ds(head, 1), :] * LOG2E
            cor = corr[pl.ds(head, 1), :]
            ph = proj[:, i * (DN + DV) : (i + 1) * (DN + DV)]
            sd = dot_t(ph, diag)
            s = sd[:, :TOK] + srot[:, j * TOK : (j + 1) * TOK]
            p = jnp.exp2(s * (SCALE * LOG2E) + (bias[part, :] - off))
            ds = (p * (sd[:, TOK:] - cor)).astype(BF16)
            pb = p.astype(BF16)
            dkv = dot_n(jnp.concatenate([ds, pb], 1), diag)
            dkvs.append((dkv * mul[...]).astype(BF16))
            dss.append(ds)
            if keep is None:
                kr = jnp.concatenate([ph[:, :DN], rope[part, :]], 1)
                dq[:, i * (DN + DR) : (i + 1) * (DN + DR)] = (dot_l(ds, kr) * SCALE).astype(BF16)
            else:
                keep(2 * i, ds)
                keep(2 * i + 1, ph[:, :DN])
        rpart = dot_n(jnp.concatenate(dss, 1), rot)
        rtotal = rpart if rtotal is None else rtotal + rpart
    racc[part, :] += rtotal
    acc[part, :] += dot_t(jnp.concatenate(dkvs, 1), w[...])


def early_kernel(
    order, member, gain, mul, offs, corr, lat, w, q, cot, stored, acc, racc, scaled, rope, bias
):
    step = pl.program_id(0)

    @pl.when(step == 0)
    def _():
        arrange((0,), order, member, gain, [lat], scaled, rope, bias)
        acc[...] = jnp.zeros_like(acc)
        racc[...] = jnp.zeros_like(racc)

    def keep(at, value):
        stored[0, at] = value

    refs = (mul, offs, corr, w, q, cot, scaled, rope, bias, acc, racc)
    heads(step, pl.ds(0, TOK), refs, keep, None)


def copy_out(step, slot, first, held, stored, sem):
    part = pl.ds(first, held.shape[2] - first)
    return pltpu.make_async_copy(
        held.at[slot, :, part], stored.at[step, :, part], sem.at[slot]
    )


def kernel(steps, order, member, gain, mul, offs, corr, *refs):
    n = len(steps)
    lats = refs[:n]
    w, q, cot, own_acc, own_racc, _, dq, stored, rope = refs[n : n + 9]
    grads = refs[n + 9 : 2 * n + 9]
    gain_rows = refs[2 * n + 9]
    scaled, bias, acc, racc, held, sem = refs[2 * n + 10 :]
    step = pl.program_id(0)
    rows = n * TOK

    @pl.when(step == 0)
    def _():
        arrange(steps, order, member, gain, lats, scaled, rope, bias)
        acc[...] = jnp.zeros_like(acc)
        racc[...] = jnp.zeros_like(racc)
        acc[pl.ds(0, TOK), :] = own_acc[...]
        racc[pl.ds(0, TOK), :] = own_racc[...]

    slot = lax.rem(step, 2)
    visitors, everyone = pl.ds(TOK, rows - TOK), pl.ds(0, rows)
    refs = (mul, offs, corr, w, q, cot, scaled, rope, bias, acc, racc)

    @pl.when(jnp.logical_and(step >= 2, step < EARLY + 2))
    def _():
        copy_out(step - 2, slot, TOK, held, stored, sem).wait()

    @pl.when(jnp.logical_and(step >= EARLY + 2, step < LATER + 2))
    def _():
        copy_out(step - 2, slot, 0, held, stored, sem).wait()

    def kept(part):
        def keep(at, value):
            held[slot, at, part, :] = value

        return keep

    @pl.when(step < EARLY)
    def _():
        heads(step, visitors, refs, kept(visitors), None)
        copy_out(step, slot, TOK, held, stored, sem).start()

    @pl.when(jnp.logical_and(step >= EARLY, step < LATER))
    def _():
        heads(step, everyone, refs, kept(everyone), None)
        copy_out(step, slot, 0, held, stored, sem).start()

    @pl.when(step >= LATER)
    def _():
        heads(step, everyone, refs, None, dq)

    @pl.when(step == H // HB - 1)
    def _():
        total = jnp.zeros((1, KVL), F32)
        for i in range(n):
            part = pl.ds(i * TOK, TOK)
            g = acc[part, :]
            tile = lats[i][:KVL, :].astype(F32).T
            total = total + jnp.sum(g * tile, axis=0, keepdims=True)
            grads[i][:KVL, :] = g.T.astype(grads[i].dtype)
            grads[i][KVL:, :] = (racc[part, :] * SCALE).T.astype(grads[i].dtype)
        gain_rows[...] = jnp.broadcast_to(total[None], gain_rows.shape)


def later_kernel(stored, rope, _, dq):
    for i in range(HB):
        kr = jnp.concatenate([stored[0, 2 * i + 1], rope[...]], 1)
        dq[:, i * (DN + DR) : (i + 1) * (DN + DR)] = (dot_l(stored[0, 2 * i], kr) * SCALE).astype(BF16)


def in_vmem(x):
    return pltpu.with_memory_space_constraint(x, pltpu.VMEM)


def later_queries(stored, rope, dq):
    rows = stored.shape[2]
    return pl.pallas_call(
        later_kernel,
        grid=(LATER,),
        out_shape=jax.ShapeDtypeStruct(dq.shape, dq.dtype),
        in_specs=[
            pl.BlockSpec((1, 2 * HB, rows, TOK), lambda i: (i, 0, 0, 0)),
            pl.BlockSpec((rows, DR), lambda i: (0, 0)),
            pl.BlockSpec(memory_space=pl.ANY),
        ],
        out_specs=pl.BlockSpec((TOK, HB * (DN + DR)), lambda i: (0, i)),
        input_output_aliases={2: 0},
        compiler_params=pltpu.CompilerParams(vmem_limit_bytes=56 * 2**20),
        cost_estimate=pl.CostEstimate(
            flops=2 * LATER * HB * TOK * rows * (DN + DR),
            bytes_accessed=LATER * HB * TOK * (4 * rows + 2 * (DN + DR)),
            transcendentals=0,
        ),
    )(stored, in_vmem(rope), dq)


def whole(*shape):
    return pl.BlockSpec(shape, lambda i: (0,) * len(shape))


def inputs_specs(n):
    sm = pl.BlockSpec(memory_space=pltpu.SMEM)
    return (
        [sm, sm, whole(1, KVL), whole(1, DN + DV), whole(H, TOK), whole(H, TOK)]
        + [whole(KVL + DR, TOK)] * n
        + [
            pl.BlockSpec((KVL, HB * (DN + DV)), lambda i: (0, i)),
            pl.BlockSpec((TOK, HB * (DN + DR)), lambda i: (0, i)),
            pl.BlockSpec((TOK, HB * DV), lambda i: (0, i)),
        ]
    )


def work(grid, rows):
    per_head = rows * (4 * KVL * (DN + DV) + 10 * TOK * DN)
    return pl.CostEstimate(
        flops=grid * HB * per_head,
        bytes_accessed=grid * HB * (2 * KVL * (DN + DV) + TOK * (4 * DN + 4 * DR)),
        transcendentals=grid * HB * rows * TOK,
    )


def early_visit(common, lat, streams):
    return pl.pallas_call(
        early_kernel,
        grid=(EARLY,),
        out_shape=[
            jax.ShapeDtypeStruct((LATER, 2 * HB, STEPS * TOK, TOK), BF16),
            pltpu.VMEM((TOK, KVL), F32),
            pltpu.VMEM((TOK, DR), F32),
        ],
        in_specs=inputs_specs(1),
        out_specs=[
            pl.BlockSpec((1, 2 * HB, TOK, TOK), lambda i: (i, 0, 0, 0)),
            whole(TOK, KVL),
            whole(TOK, DR),
        ],
        scratch_shapes=[
            pltpu.VMEM((TOK, KVL), BF16),
            pltpu.VMEM((TOK, DR), BF16),
            pltpu.VMEM((TOK, TOK), F32),
        ],
        compiler_params=pltpu.CompilerParams(vmem_limit_bytes=56 * 2**20),
        cost_estimate=work(EARLY, TOK),
    )(*common, lat, *streams)


def visits(steps, common, lats, streams, early, peers):
    n = len(steps)
    rows = n * TOK
    anywhere = pl.BlockSpec(memory_space=pl.ANY)
    stored, own_acc, own_racc = early
    return pl.pallas_call(
        functools.partial(kernel, steps),
        grid=(H // HB,),
        out_shape=[
            jax.ShapeDtypeStruct((TOK, H * (DN + DR)), BF16),
            jax.ShapeDtypeStruct(stored.shape, BF16),
            pltpu.VMEM((rows, DR), BF16),
        ]
        + [jax.ShapeDtypeStruct((KVL + DR, TOK), F32)]
        + [pltpu.VMEM((KVL + DR, TOK), BF16)] * (n - 1)
        + [jax.ShapeDtypeStruct((peers, 1, KVL), F32)],
        in_specs=inputs_specs(n) + [whole(TOK, KVL), whole(TOK, DR), anywhere],
        out_specs=[
            pl.BlockSpec((TOK, HB * (DN + DR)), lambda i: (0, jnp.maximum(i, LATER))),
            anywhere,
            whole(rows, DR),
        ]
        + [whole(KVL + DR, TOK)] * n
        + [whole(peers, 1, KVL)],
        scratch_shapes=[
            pltpu.VMEM((rows, KVL), BF16),
            pltpu.VMEM((rows, TOK), F32),
            pltpu.VMEM((rows, KVL), F32),
            pltpu.VMEM((rows, DR), F32),
            pltpu.VMEM((2, 2 * HB, rows, TOK), BF16),
            pltpu.SemaphoreType.DMA((2,)),
        ],
        input_output_aliases={6 + n + 5: 1},
        compiler_params=pltpu.CompilerParams(vmem_limit_bytes=56 * 2**20),
        cost_estimate=work(H // HB, rows),
    )(
        *common,
        lats[0],
        *map(in_vmem, lats[1:]),
        *streams,
        in_vmem(own_acc),
        in_vmem(own_racc),
        stored,
    )


def everywhere_sum(rows):
    moved_rows = lax.all_to_all(rows, ("ctx", "dp"), 0, 0, tiled=True)
    return jnp.sum(moved_rows, (0, 1))


def moved(x, distance):
    n = lax.axis_size("ctx")
    return lax.ppermute(x, "ctx", [((i - distance) % n, i) for i in range(n)])


def body(queries, latents, cotangent, offsets, corrections, span_order, latent_gain, up_weight):
    own = latents[0].T
    member = lax.axis_index("ctx").astype(jnp.int32).reshape(1)
    lats = [own] + [moved(own, s) for s in range(1, STEPS)]
    mul = jnp.concatenate([jnp.full((1, DN), SCALE, F32), jnp.ones((1, DV), F32)], 1)
    common = (span_order, member, latent_gain[None], mul, offsets[0], corrections[0])
    streams = (up_weight, queries[0], cotangent[0])
    early = early_visit(common, own, streams)
    peers = lax.axis_size("ctx") * lax.axis_size("dp")
    dq, stored, rope, *grads, gain_rows = visits(
        tuple(range(STEPS)), common, lats, streams, early, peers
    )
    back = [moved(grads[s], -s) for s in range(1, STEPS)]
    gain_sum = everywhere_sum(gain_rows)
    dq = later_queries(stored, rope, dq)
    back = [b.astype(F32) for b in back]
    total = grads[0] + ((back[0] + back[1]) + (back[2] + back[3]))
    factor = jnp.concatenate([latent_gain, jnp.ones((DR,), F32)])
    return dq[None], (total * factor[:, None]).T[None], gain_sum


def solution(mesh):
    in_specs = (
        P("dp", "ctx", None),
        P("dp", "ctx", None),
        P("dp", "ctx", None),
        P("dp", None, "ctx"),
        P("dp", None, "ctx"),
        P("dp", None),
        P(),
        P(),
    )
    out_specs = (P("dp", "ctx", None), P("dp", "ctx", None), P())
    return jax.shard_map(body, mesh=mesh, in_specs=in_specs, out_specs=out_specs, check_vma=False)
```

```python
import functools
import jax
import jax.numpy as jnp
from jax import lax
from jax.experimental import pallas as pl
from jax.experimental.pallas import tpu as pltpu
from jax.sharding import PartitionSpec as P

H = 64
KVL = 512
DR = 64
DN = 128
DV = 128
STEPS = 5
HB = 8
LATER = 6
EARLY = 3
PARTS = 4
TOK = 128
N_CTX = 32
SCALE = (DN + DR) ** -0.5
LOG2E = 1.4426950408889634
F32 = jnp.float32
BF16 = jnp.bfloat16


def dot_t(a, b):
    return lax.dot_general(a, b, (((1,), (1,)), ((), ())), preferred_element_type=F32)


def dot_l(a, b):
    return lax.dot_general(a, b, (((0,), (0,)), ((), ())), preferred_element_type=F32)


def dot_n(a, b):
    return jnp.dot(a, b, preferred_element_type=F32)


def arrange(steps, order, member, gain, lats, scaled, rope, bias):
    half = TOK // 2
    rows = lax.broadcasted_iota(jnp.int32, (TOK, TOK), 0)
    cols = lax.broadcasted_iota(jnp.int32, (TOK, TOK), 1)
    own = member[0]

    def positions(index, group):
        block = jnp.where(index < half, order[0, 2 * group], order[0, 2 * group + 1])
        return block * half + lax.rem(index, half)

    qpos = positions(cols, own)
    for i, s in enumerate(steps):
        group = lax.rem(own + N_CTX - s, N_CTX)
        kpos = positions(rows, group)
        part = pl.ds(i * TOK, TOK)
        bias[part, :] = jnp.where(kpos <= qpos, 0.0, -1e30)
        tile = lats[i][...].astype(F32).T
        scaled[part, :] = (tile[:, :KVL] * gain[...]).astype(BF16)
        rope[part, :] = tile[:, KVL:].astype(BF16)


def heads(step, part, refs, keep, dq):
    mul, offs, corr, w, q, cot, scaled, rope, bias, acc, racc = refs
    zero = jnp.zeros((TOK, TOK), BF16)
    proj = dot_n(scaled[part, :], w[...]).astype(BF16)
    dkvs, all_ds, rots = [], [], []
    for pair in range(HB // 2):
        base = 2 * pair * (DN + DR)
        rot = jnp.concatenate(
            [q[:, base + DN : base + DN + DR], q[:, base + 2 * DN + DR : base + 2 * (DN + DR)]], 0
        )
        rots.append(rot)
        srot = dot_t(rope[part, :], rot)
        both = (2 * pair, 2 * pair + 1)
        diags, phs, sds, dss, pbs = [], [], [], [], []
        for i in both:
            qn = q[:, i * (DN + DR) : i * (DN + DR) + DN]
            ct = cot[:, i * DV : (i + 1) * DV]
            diags.append(
                jnp.concatenate(
                    [jnp.concatenate([qn, zero], 1), jnp.concatenate([zero, ct], 1)], 0
                )
            )
            phs.append(proj[:, i * (DN + DV) : (i + 1) * (DN + DV)])
            sds.append(dot_t(phs[-1], diags[-1]))
        for j, i in enumerate(both):
            head = step * HB + i
            off = offs[pl.ds(head, 1), :] * LOG2E
            cor = corr[pl.ds(head, 1), :]
            s = sds[j][:, :TOK] + srot[:, j * TOK : (j + 1) * TOK]
            p = jnp.exp2(s * (SCALE * LOG2E) + (bias[part, :] - off))
            dss.append((p * (sds[j][:, TOK:] - cor)).astype(BF16))
            pbs.append(p.astype(BF16))
        for j, i in enumerate(both):
            dkv = dot_n(jnp.concatenate([dss[j], pbs[j]], 1), diags[j])
            dkvs.append((dkv * mul[...]).astype(BF16))
            if keep is None:
                kr = jnp.concatenate([phs[j][:, :DN], rope[part, :]], 1)
                dq[:, i * (DN + DR) : (i + 1) * (DN + DR)] = (dot_l(dss[j], kr) * SCALE).astype(BF16)
            else:
                keep(i, dss[j])
                keep(HB + i, phs[j][:, :DN])
        all_ds += dss
    racc[part, :] += dot_n(jnp.concatenate(all_ds, 1), jnp.concatenate(rots, 0))
    acc[part, :] += dot_t(jnp.concatenate(dkvs, 1), w[...])


def early_kernel(
    order, member, gain, mul, offs, corr, lat, w, q, cot, stored, acc, racc, scaled, rope, bias
):
    step = pl.program_id(0)

    @pl.when(step == 0)
    def _():
        arrange((0,), order, member, gain, [lat], scaled, rope, bias)
        acc[...] = jnp.zeros_like(acc)
        racc[...] = jnp.zeros_like(racc)

    def keep(at, value):
        stored[0, at] = value

    refs = (mul, offs, corr, w, q, cot, scaled, rope, bias, acc, racc)
    heads(step, pl.ds(0, TOK), refs, keep, None)


def copy_out(step, slot, first, held, stored, sem):
    part = pl.ds(first, held.shape[2] - first)
    return pltpu.make_async_copy(
        held.at[slot, :, part], stored.at[step, :, part], sem.at[slot]
    )


def kernel(steps, order, member, gain, mul, offs, corr, *refs):
    n = len(steps)
    lats = refs[:n]
    w, q, cot, own_acc, own_racc, _, dq, stored, rope = refs[n : n + 9]
    grads = refs[n + 9 : 2 * n + 9]
    gain_rows = refs[2 * n + 9]
    scaled, bias, acc, racc, held, sem = refs[2 * n + 10 :]
    step = pl.program_id(0)
    rows = n * TOK

    @pl.when(step == 0)
    def _():
        arrange(steps, order, member, gain, lats, scaled, rope, bias)
        acc[...] = jnp.zeros_like(acc)
        racc[...] = jnp.zeros_like(racc)
        acc[pl.ds(0, TOK), :] = own_acc[...]
        racc[pl.ds(0, TOK), :] = own_racc[...]

    slot = lax.rem(step, 2)
    visitors, everyone = pl.ds(TOK, rows - TOK), pl.ds(0, rows)
    refs = (mul, offs, corr, w, q, cot, scaled, rope, bias, acc, racc)

    @pl.when(jnp.logical_and(step >= 2, step < EARLY + 2))
    def _():
        copy_out(step - 2, slot, TOK, held, stored, sem).wait()

    @pl.when(jnp.logical_and(step >= EARLY + 2, step < LATER + 2))
    def _():
        copy_out(step - 2, slot, 0, held, stored, sem).wait()

    def kept(part):
        def keep(at, value):
            held[slot, at, part, :] = value

        return keep

    @pl.when(step < EARLY)
    def _():
        heads(step, visitors, refs, kept(visitors), None)
        copy_out(step, slot, TOK, held, stored, sem).start()

    @pl.when(jnp.logical_and(step >= EARLY, step < LATER))
    def _():
        heads(step, everyone, refs, kept(everyone), None)
        copy_out(step, slot, 0, held, stored, sem).start()

    @pl.when(step >= LATER)
    def _():
        heads(step, everyone, refs, None, dq)

    @pl.when(step == H // HB - 1)
    def _():
        total = jnp.zeros((1, KVL), F32)
        for i in range(n):
            part = pl.ds(i * TOK, TOK)
            g = acc[part, :]
            tile = lats[i][:KVL, :].astype(F32).T
            total = total + jnp.sum(g * tile, axis=0, keepdims=True)
            grads[i][:KVL, :] = g.T.astype(grads[i].dtype)
            grads[i][KVL:, :] = (racc[part, :] * SCALE).T.astype(grads[i].dtype)
        gain_rows[...] = jnp.broadcast_to(total[None], gain_rows.shape)


def later_kernel(*refs):
    rope, _, dq = refs[PARTS:]
    each = 2 * HB // PARTS
    for i in range(HB):
        ds = refs[i // each][0, i % each]
        keys = refs[(HB + i) // each][0, i % each]
        kr = jnp.concatenate([keys, rope[...]], 1)
        dq[:, i * (DN + DR) : (i + 1) * (DN + DR)] = (dot_l(ds, kr) * SCALE).astype(BF16)


def in_vmem(x):
    return pltpu.with_memory_space_constraint(x, pltpu.VMEM)


def stored_part(part, i):
    return i, part, 0, 0


def later_queries(stored, rope, dq):
    rows = stored.shape[2]
    return pl.pallas_call(
        later_kernel,
        grid=(LATER,),
        out_shape=jax.ShapeDtypeStruct(dq.shape, dq.dtype),
        in_specs=[
            *[
                pl.BlockSpec((1, 2 * HB // PARTS, rows, TOK), functools.partial(stored_part, j))
                for j in range(PARTS)
            ],
            pl.BlockSpec((rows, DR), lambda i: (0, 0)),
            pl.BlockSpec(memory_space=pl.ANY),
        ],
        out_specs=pl.BlockSpec((TOK, HB * (DN + DR)), lambda i: (0, i)),
        input_output_aliases={PARTS + 1: 0},
        compiler_params=pltpu.CompilerParams(vmem_limit_bytes=56 * 2**20),
        cost_estimate=pl.CostEstimate(
            flops=2 * LATER * HB * TOK * rows * (DN + DR),
            bytes_accessed=LATER * HB * TOK * (4 * rows + 2 * (DN + DR)),
            transcendentals=0,
        ),
    )(*[stored] * PARTS, in_vmem(rope), dq)


def whole(*shape):
    return pl.BlockSpec(shape, lambda i: (0,) * len(shape))


def inputs_specs(n):
    sm = pl.BlockSpec(memory_space=pltpu.SMEM)
    return (
        [sm, sm, whole(1, KVL), whole(1, DN + DV), whole(H, TOK), whole(H, TOK)]
        + [whole(KVL + DR, TOK)] * n
        + [
            pl.BlockSpec((KVL, HB * (DN + DV)), lambda i: (0, i)),
            pl.BlockSpec((TOK, HB * (DN + DR)), lambda i: (0, i)),
            pl.BlockSpec((TOK, HB * DV), lambda i: (0, i)),
        ]
    )


def work(grid, rows):
    per_head = rows * (4 * KVL * (DN + DV) + 10 * TOK * DN)
    return pl.CostEstimate(
        flops=grid * HB * per_head,
        bytes_accessed=grid * HB * (2 * KVL * (DN + DV) + TOK * (4 * DN + 4 * DR)),
        transcendentals=grid * HB * rows * TOK,
    )


def early_visit(common, lat, streams):
    return pl.pallas_call(
        early_kernel,
        grid=(EARLY,),
        out_shape=[
            jax.ShapeDtypeStruct((LATER, 2 * HB, STEPS * TOK, TOK), BF16),
            pltpu.VMEM((TOK, KVL), F32),
            pltpu.VMEM((TOK, DR), F32),
        ],
        in_specs=inputs_specs(1),
        out_specs=[
            pl.BlockSpec((1, 2 * HB, TOK, TOK), lambda i: (i, 0, 0, 0)),
            whole(TOK, KVL),
            whole(TOK, DR),
        ],
        scratch_shapes=[
            pltpu.VMEM((TOK, KVL), BF16),
            pltpu.VMEM((TOK, DR), BF16),
            pltpu.VMEM((TOK, TOK), F32),
        ],
        compiler_params=pltpu.CompilerParams(vmem_limit_bytes=56 * 2**20),
        cost_estimate=work(EARLY, TOK),
    )(*common, lat, *streams)


def visits(steps, common, lats, streams, early, peers):
    n = len(steps)
    rows = n * TOK
    anywhere = pl.BlockSpec(memory_space=pl.ANY)
    stored, own_acc, own_racc = early
    return pl.pallas_call(
        functools.partial(kernel, steps),
        grid=(H // HB,),
        out_shape=[
            jax.ShapeDtypeStruct((TOK, H * (DN + DR)), BF16),
            jax.ShapeDtypeStruct(stored.shape, BF16),
            pltpu.VMEM((rows, DR), BF16),
        ]
        + [jax.ShapeDtypeStruct((KVL + DR, TOK), F32)]
        + [pltpu.VMEM((KVL + DR, TOK), BF16)] * (n - 1)
        + [jax.ShapeDtypeStruct((peers, 1, KVL), F32)],
        in_specs=inputs_specs(n) + [whole(TOK, KVL), whole(TOK, DR), anywhere],
        out_specs=[
            pl.BlockSpec((TOK, HB * (DN + DR)), lambda i: (0, jnp.maximum(i, LATER))),
            anywhere,
            whole(rows, DR),
        ]
        + [whole(KVL + DR, TOK)] * n
        + [whole(peers, 1, KVL)],
        scratch_shapes=[
            pltpu.VMEM((rows, KVL), BF16),
            pltpu.VMEM((rows, TOK), F32),
            pltpu.VMEM((rows, KVL), F32),
            pltpu.VMEM((rows, DR), F32),
            pltpu.VMEM((2, 2 * HB, rows, TOK), BF16),
            pltpu.SemaphoreType.DMA((2,)),
        ],
        input_output_aliases={6 + n + 5: 1},
        compiler_params=pltpu.CompilerParams(vmem_limit_bytes=56 * 2**20),
        cost_estimate=work(H // HB, rows),
    )(
        *common,
        lats[0],
        *map(in_vmem, lats[1:]),
        *streams,
        in_vmem(own_acc),
        in_vmem(own_racc),
        stored,
    )


def everywhere_sum(rows):
    moved_rows = lax.all_to_all(rows, ("ctx", "dp"), 0, 0, tiled=True)
    return jnp.sum(moved_rows, (0, 1))


def moved(x, distance):
    n = lax.axis_size("ctx")
    return lax.ppermute(x, "ctx", [((i - distance) % n, i) for i in range(n)])


def body(queries, latents, cotangent, offsets, corrections, span_order, latent_gain, up_weight):
    own = latents[0].T
    member = lax.axis_index("ctx").astype(jnp.int32).reshape(1)
    lats = [own] + [moved(own, s) for s in range(1, STEPS)]
    mul = jnp.concatenate([jnp.full((1, DN), SCALE, F32), jnp.ones((1, DV), F32)], 1)
    common = (span_order, member, latent_gain[None], mul, offsets[0], corrections[0])
    streams = (up_weight, queries[0], cotangent[0])
    early = early_visit(common, own, streams)
    peers = lax.axis_size("ctx") * lax.axis_size("dp")
    dq, stored, rope, *grads, gain_rows = visits(
        tuple(range(STEPS)), common, lats, streams, early, peers
    )
    back = [moved(grads[s], -s) for s in range(1, STEPS)]
    gain_sum = everywhere_sum(gain_rows)
    dq = later_queries(stored, rope, dq)
    back = [b.astype(F32) for b in back]
    total = grads[0] + ((back[0] + back[1]) + (back[2] + back[3]))
    factor = jnp.concatenate([latent_gain, jnp.ones((DR,), F32)])
    return dq[None], (total * factor[:, None]).T[None], gain_sum


def solution(mesh):
    in_specs = (
        P("dp", "ctx", None),
        P("dp", "ctx", None),
        P("dp", "ctx", None),
        P("dp", None, "ctx"),
        P("dp", None, "ctx"),
        P("dp", None),
        P(),
        P(),
    )
    out_specs = (P("dp", "ctx", None), P("dp", "ctx", None), P())
    return jax.shard_map(body, mesh=mesh, in_specs=in_specs, out_specs=out_specs, check_vma=False)
```

```python
import functools
import jax
import jax.numpy as jnp
from jax import lax
from jax.experimental import pallas as pl
from jax.experimental.pallas import tpu as pltpu
from jax.sharding import PartitionSpec as P

H = 64
KVL = 512
DR = 64
DN = 128
DV = 128
STEPS = 5
HB = 8
LATER = 6
EARLY = 3
PARTS = 4
TOK = 128
N_CTX = 32
SCALE = (DN + DR) ** -0.5
LOG2E = 1.4426950408889634
F32 = jnp.float32
BF16 = jnp.bfloat16


def dot_t(a, b):
    return lax.dot_general(a, b, (((1,), (1,)), ((), ())), preferred_element_type=F32)


def dot_l(a, b):
    return lax.dot_general(a, b, (((0,), (0,)), ((), ())), preferred_element_type=F32)


def dot_n(a, b):
    return jnp.dot(a, b, preferred_element_type=F32)


def arrange(steps, order, member, gain, lats, scaled, rope, bias):
    half = TOK // 2
    rows = lax.broadcasted_iota(jnp.int32, (TOK, TOK), 0)
    cols = lax.broadcasted_iota(jnp.int32, (TOK, TOK), 1)
    own = member[0]

    def positions(index, group):
        block = jnp.where(index < half, order[0, 2 * group], order[0, 2 * group + 1])
        return block * half + lax.rem(index, half)

    qpos = positions(cols, own)
    for i, s in enumerate(steps):
        group = lax.rem(own + N_CTX - s, N_CTX)
        kpos = positions(rows, group)
        part = pl.ds(i * TOK, TOK)
        bias[part, :] = jnp.where(kpos <= qpos, 0.0, -1e30)
        tile = lats[i][...].astype(F32).T
        scaled[part, :] = (tile[:, :KVL] * gain[...]).astype(BF16)
        rope[part, :] = tile[:, KVL:].astype(BF16)


def heads(step, part, refs, keep, dq):
    mul, offs, corr, w, q, cot, scaled, rope, bias, acc, racc = refs
    zero = jnp.zeros((TOK, TOK), BF16)
    proj = dot_n(scaled[part, :], w[...]).astype(BF16)
    dkvs, all_ds, rots = [], [], []
    for pair in range(HB // 2):
        base = 2 * pair * (DN + DR)
        rot = jnp.concatenate(
            [q[:, base + DN : base + DN + DR], q[:, base + 2 * DN + DR : base + 2 * (DN + DR)]], 0
        )
        rots.append(rot)
        srot = dot_t(rope[part, :], rot)
        both = (2 * pair, 2 * pair + 1)
        diags, phs, sds, dss, pbs = [], [], [], [], []
        for i in both:
            qn = q[:, i * (DN + DR) : i * (DN + DR) + DN]
            ct = cot[:, i * DV : (i + 1) * DV]
            diags.append(
                jnp.concatenate(
                    [jnp.concatenate([qn, zero], 1), jnp.concatenate([zero, ct], 1)], 0
                )
            )
            phs.append(proj[:, i * (DN + DV) : (i + 1) * (DN + DV)])
            sds.append(dot_t(phs[-1], diags[-1]))
        for j, i in enumerate(both):
            head = step * HB + i
            off = offs[pl.ds(head, 1), :] * LOG2E
            cor = corr[pl.ds(head, 1), :]
            s = sds[j][:, :TOK] + srot[:, j * TOK : (j + 1) * TOK]
            p = jnp.exp2(s * (SCALE * LOG2E) + (bias[part, :] - off))
            dss.append((p * (sds[j][:, TOK:] - cor)).astype(BF16))
            pbs.append(p.astype(BF16))
        for j, i in enumerate(both):
            dkv = dot_n(jnp.concatenate([dss[j], pbs[j]], 1), diags[j])
            dkvs.append((dkv * mul[...]).astype(BF16))
            if keep is None:
                kr = jnp.concatenate([phs[j][:, :DN], rope[part, :]], 1)
                dq[:, i * (DN + DR) : (i + 1) * (DN + DR)] = (dot_l(dss[j], kr) * SCALE).astype(BF16)
            else:
                keep(i, dss[j])
                keep(HB + i, phs[j][:, :DN])
        all_ds += dss
    racc[part, :] += dot_n(jnp.concatenate(all_ds, 1), jnp.concatenate(rots, 0))
    acc[part, :] += dot_t(jnp.concatenate(dkvs, 1), w[...])


def early_kernel(
    order, member, gain, mul, offs, corr, lat, w, q, cot, stored, acc, racc, scaled, rope, bias
):
    step = pl.program_id(0)

    @pl.when(step == 0)
    def _():
        arrange((0,), order, member, gain, [lat], scaled, rope, bias)
        acc[...] = jnp.zeros_like(acc)
        racc[...] = jnp.zeros_like(racc)

    def keep(at, value):
        stored[0, at] = value

    refs = (mul, offs, corr, w, q, cot, scaled, rope, bias, acc, racc)
    heads(step, pl.ds(0, TOK), refs, keep, None)


def copy_out(step, slot, first, held, stored, sem):
    part = pl.ds(first, held.shape[2] - first)
    return pltpu.make_async_copy(
        held.at[slot, :, part], stored.at[step, :, part], sem.at[slot]
    )


def kernel(steps, order, member, gain, mul, offs, corr, *refs):
    n = len(steps)
    lats = refs[:n]
    w, q, cot, own_acc, own_racc, _, dq, stored, rope = refs[n : n + 9]
    grads = refs[n + 9 : 2 * n + 9]
    gain_rows = refs[2 * n + 9]
    scaled, bias, acc, racc, held, sem = refs[2 * n + 10 :]
    step = pl.program_id(0)
    rows = n * TOK

    @pl.when(step == 0)
    def _():
        arrange(steps, order, member, gain, lats, scaled, rope, bias)
        acc[...] = jnp.zeros_like(acc)
        racc[...] = jnp.zeros_like(racc)
        acc[pl.ds(0, TOK), :] = own_acc[...]
        racc[pl.ds(0, TOK), :] = own_racc[...]

    slot = lax.rem(step, 2)
    visitors, everyone = pl.ds(TOK, rows - TOK), pl.ds(0, rows)
    refs = (mul, offs, corr, w, q, cot, scaled, rope, bias, acc, racc)

    @pl.when(jnp.logical_and(step >= 2, step < EARLY + 2))
    def _():
        copy_out(step - 2, slot, TOK, held, stored, sem).wait()

    @pl.when(jnp.logical_and(step >= EARLY + 2, step < LATER + 2))
    def _():
        copy_out(step - 2, slot, 0, held, stored, sem).wait()

    def kept(part):
        def keep(at, value):
            held[slot, at, part, :] = value

        return keep

    @pl.when(step < EARLY)
    def _():
        heads(step, visitors, refs, kept(visitors), None)
        copy_out(step, slot, TOK, held, stored, sem).start()

    @pl.when(jnp.logical_and(step >= EARLY, step < LATER))
    def _():
        heads(step, everyone, refs, kept(everyone), None)
        copy_out(step, slot, 0, held, stored, sem).start()

    @pl.when(step >= LATER)
    def _():
        heads(step, everyone, refs, None, dq)

    @pl.when(step == H // HB - 1)
    def _():
        total = jnp.zeros((1, KVL), F32)
        for i in range(n):
            part = pl.ds(i * TOK, TOK)
            g = acc[part, :]
            tile = lats[i][:KVL, :].astype(F32).T
            total = total + jnp.sum(g * tile, axis=0, keepdims=True)
            grads[i][:KVL, :] = g.T.astype(grads[i].dtype)
            grads[i][KVL:, :] = (racc[part, :] * SCALE).T.astype(grads[i].dtype)
        gain_rows[...] = jnp.broadcast_to(total[None], gain_rows.shape)


def later_kernel(*refs):
    rope, _, dq = refs[PARTS:]
    each = 2 * HB // PARTS
    for i in range(HB):
        ds = refs[i // each][0, i % each]
        keys = refs[(HB + i) // each][0, i % each]
        kr = jnp.concatenate([keys, rope[...]], 1)
        dq[:, i * (DN + DR) : (i + 1) * (DN + DR)] = (dot_l(ds, kr) * SCALE).astype(BF16)


def in_vmem(x):
    return pltpu.with_memory_space_constraint(x, pltpu.VMEM)


def stored_part(part, i):
    return i, part, 0, 0


def later_queries(stored, rope, dq):
    rows = stored.shape[2]
    return pl.pallas_call(
        later_kernel,
        grid=(LATER,),
        out_shape=jax.ShapeDtypeStruct(dq.shape, dq.dtype),
        in_specs=[
            *[
                pl.BlockSpec((1, 2 * HB // PARTS, rows, TOK), functools.partial(stored_part, j))
                for j in range(PARTS)
            ],
            pl.BlockSpec((rows, DR), lambda i: (0, 0)),
            pl.BlockSpec(memory_space=pl.ANY),
        ],
        out_specs=pl.BlockSpec((TOK, HB * (DN + DR)), lambda i: (0, i)),
        input_output_aliases={PARTS + 1: 0},
        compiler_params=pltpu.CompilerParams(vmem_limit_bytes=56 * 2**20),
        cost_estimate=pl.CostEstimate(
            flops=2 * LATER * HB * TOK * rows * (DN + DR),
            bytes_accessed=LATER * HB * TOK * (4 * rows + 2 * (DN + DR)),
            transcendentals=0,
        ),
    )(*[stored] * PARTS, in_vmem(rope), dq)


def whole(*shape):
    return pl.BlockSpec(shape, lambda i: (0,) * len(shape))


def inputs_specs(n):
    sm = pl.BlockSpec(memory_space=pltpu.SMEM)
    return (
        [sm, sm, whole(1, KVL), whole(1, DN + DV), whole(H, TOK), whole(H, TOK)]
        + [whole(KVL + DR, TOK)] * n
        + [
            pl.BlockSpec((KVL, HB * (DN + DV)), lambda i: (0, i)),
            pl.BlockSpec((TOK, HB * (DN + DR)), lambda i: (0, i)),
            pl.BlockSpec((TOK, HB * DV), lambda i: (0, i)),
        ]
    )


def work(grid, rows):
    per_head = rows * (4 * KVL * (DN + DV) + 10 * TOK * DN)
    return pl.CostEstimate(
        flops=grid * HB * per_head,
        bytes_accessed=grid * HB * (2 * KVL * (DN + DV) + TOK * (4 * DN + 4 * DR)),
        transcendentals=grid * HB * rows * TOK,
    )


def early_visit(common, lat, streams):
    return pl.pallas_call(
        early_kernel,
        grid=(EARLY,),
        out_shape=[
            jax.ShapeDtypeStruct((LATER, 2 * HB, STEPS * TOK, TOK), BF16),
            pltpu.VMEM((TOK, KVL), F32),
            pltpu.VMEM((TOK, DR), F32),
        ],
        in_specs=inputs_specs(1),
        out_specs=[
            pl.BlockSpec((1, 2 * HB, TOK, TOK), lambda i: (i, 0, 0, 0)),
            whole(TOK, KVL),
            whole(TOK, DR),
        ],
        scratch_shapes=[
            pltpu.VMEM((TOK, KVL), BF16),
            pltpu.VMEM((TOK, DR), BF16),
            pltpu.VMEM((TOK, TOK), F32),
        ],
        compiler_params=pltpu.CompilerParams(vmem_limit_bytes=56 * 2**20),
        cost_estimate=work(EARLY, TOK),
    )(*common, lat, *streams)


def visits(steps, common, lats, streams, early, peers):
    n = len(steps)
    rows = n * TOK
    anywhere = pl.BlockSpec(memory_space=pl.ANY)
    stored, own_acc, own_racc = early
    return pl.pallas_call(
        functools.partial(kernel, steps),
        grid=(H // HB,),
        out_shape=[
            jax.ShapeDtypeStruct((TOK, H * (DN + DR)), BF16),
            jax.ShapeDtypeStruct(stored.shape, BF16),
            pltpu.VMEM((rows, DR), BF16),
        ]
        + [pltpu.VMEM((KVL + DR, TOK), F32)]
        + [pltpu.VMEM((KVL + DR, TOK), BF16)] * (n - 1)
        + [pltpu.VMEM((peers, 1, KVL), F32)],
        in_specs=inputs_specs(n) + [whole(TOK, KVL), whole(TOK, DR), anywhere],
        out_specs=[
            pl.BlockSpec((TOK, HB * (DN + DR)), lambda i: (0, jnp.maximum(i, LATER))),
            anywhere,
            whole(rows, DR),
        ]
        + [whole(KVL + DR, TOK)] * n
        + [whole(peers, 1, KVL)],
        scratch_shapes=[
            pltpu.VMEM((rows, KVL), BF16),
            pltpu.VMEM((rows, TOK), F32),
            pltpu.VMEM((rows, KVL), F32),
            pltpu.VMEM((rows, DR), F32),
            pltpu.VMEM((2, 2 * HB, rows, TOK), BF16),
            pltpu.SemaphoreType.DMA((2,)),
        ],
        input_output_aliases={6 + n + 5: 1},
        compiler_params=pltpu.CompilerParams(vmem_limit_bytes=56 * 2**20),
        cost_estimate=work(H // HB, rows),
    )(
        *common,
        lats[0],
        *map(in_vmem, lats[1:]),
        *streams,
        in_vmem(own_acc),
        in_vmem(own_racc),
        stored,
    )


def everywhere_sum(rows):
    moved_rows = lax.all_to_all(rows, ("ctx", "dp"), 0, 0, tiled=True)
    return jnp.sum(moved_rows, (0, 1))


def moved(x, distance):
    n = lax.axis_size("ctx")
    return lax.ppermute(x, "ctx", [((i - distance) % n, i) for i in range(n)])


def body(queries, latents, cotangent, offsets, corrections, span_order, latent_gain, up_weight):
    own = latents[0].T
    member = lax.axis_index("ctx").astype(jnp.int32).reshape(1)
    lats = [own] + [moved(own, s) for s in range(1, STEPS)]
    mul = jnp.concatenate([jnp.full((1, DN), SCALE, F32), jnp.ones((1, DV), F32)], 1)
    common = (span_order, member, latent_gain[None], mul, offsets[0], corrections[0])
    streams = (up_weight, queries[0], cotangent[0])
    early = early_visit(common, own, streams)
    peers = lax.axis_size("ctx") * lax.axis_size("dp")
    dq, stored, rope, *grads, gain_rows = visits(
        tuple(range(STEPS)), common, lats, streams, early, peers
    )
    back = [moved(grads[s], -s) for s in range(1, STEPS)]
    gain_sum = everywhere_sum(gain_rows)
    dq = later_queries(stored, rope, dq)
    back = [b.astype(F32) for b in back]
    total = grads[0] + ((back[0] + back[1]) + (back[2] + back[3]))
    factor = jnp.concatenate([latent_gain, jnp.ones((DR,), F32)])
    return dq[None], (total * factor[:, None]).T[None], gain_sum


def solution(mesh):
    in_specs = (
        P("dp", "ctx", None),
        P("dp", "ctx", None),
        P("dp", "ctx", None),
        P("dp", None, "ctx"),
        P("dp", None, "ctx"),
        P("dp", None),
        P(),
        P(),
    )
    out_specs = (P("dp", "ctx", None), P("dp", "ctx", None), P())
    return jax.shard_map(body, mesh=mesh, in_specs=in_specs, out_specs=out_specs, check_vma=False)
```
